32 devices in a mesh: groups: 2 (over y), hidden: 4 (over z), width: 4 (over x, core).
Axes of the slice: x: 2, y: 2, z: 4, core: 2. Of those that a mesh axis runs over, the one named last changes fastest.
Arguments:
- tokens: bfloat16 [64, 12288], P(('groups', 'hidden'), 'width'), parts along dimension 0, may hold values from -6 to 6
- w_in: bfloat16 [12288, 24576], P('width', 'hidden'), may hold values from -0.0546875 to 0.0546875
- w_out: bfloat16 [24576, 12288], P('hidden', 'width'), may hold values from -0.0546875 to 0.0546875
Outputs:
- result_state: bfloat16 [64, 12288], P(('groups', 'hidden'), 'width'), parts along dimension 0
The draws below stay inside these ranges and needn't reach their ends.
There are 2 independent parts, one for each index of `groups`. The reference program is written for one: setup_inputs(seed, part) draws one part's arguments, and reference() takes and returns one part's arrays. A program takes and returns all parts, laid end to end along the dimension named above; an argument that names none is the same for every part. Nothing has to cross between parts.
All inputs are finite; a program needn't handle non-finite values.
Results may differ from the reference program's by a relative error of at most 0.018.
Values may be sent and summed in bfloat16 or wider, within the bound.
No kernel may reach another device: no remote copies, remote signals or barrier semaphores. Data moves between devices by JAX's collectives and lax.ppermute only.
A program may use at most 192 MiB of HBM per device.

```python
import jax
import jax.numpy as jnp

D = 12288
FF = 24576
STEPS = 2
ROWS = 32


def strengthened(values, own_key, source, target, shards_of, factor):
    def block_of(dim):
        return (jnp.arange(values.shape[dim]) // (values.shape[dim] // shards_of)).reshape((-1,) + (1,) * (values.ndim - 1 - dim))

    one_side = jax.random.permutation(own_key, shards_of)[block_of(target)]
    second = (block_of(target) + shards_of // 2) % shards_of
    return jnp.where((block_of(source) == one_side) | (block_of(source) == second), factor * values, values)


def block_scale(key, shape, shards, smallest, largest):
    def one(position, blocks):
        steps = jax.random.uniform(jax.random.fold_in(jax.random.fold_in(key, 6), position), (blocks,), jnp.float32, smallest / len(shards), largest / len(shards))
        return jnp.repeat(jnp.exp(steps), shape[position] // blocks).reshape((-1,) + (1,) * (len(shape) - position - 1))

    level = one(*shards[0])
    for cut in shards[1:]:
        level = level * one(*cut)
    return level


def normal_values(stream_key, shape, width, bound, split=(), kind=jnp.bfloat16):
    drawn = jax.random.normal(stream_key, shape, jnp.float32) * width
    if len(split) > 0:
        drawn = block_scale(stream_key, shape, split, -0.22, 0.18) * drawn
    return jnp.clip(drawn, min=-bound, max=bound).astype(kind)


def heavy_noise(own_key, extent, deviation, most, cuts, heavy, kind=jnp.bfloat16):
    values = deviation * jax.random.normal(own_key, extent, jnp.float32)
    if cuts:
        values = values * block_scale(own_key, extent, cuts, -0.22, 0.18)
    return jnp.clip(strengthened(values, jax.random.fold_in(own_key, 3), *heavy), -most, most).astype(kind)


def setup_inputs(seed: int = 0, part: int = 0) -> dict:
    splits = jax.random.split(jax.random.key(seed), 4)
    own_keys = jax.random.split(jax.random.fold_in(splits[3], part), 4)
    return {
        "tokens": normal_values(own_keys[0], (ROWS, D), 1.0, 6.0, ((0, 4), (1, 4))),
        "w_in": normal_values(splits[1], (D, FF), D ** -0.5, 0.0546875, ((0, 4), (1, 4))),
        "w_out": heavy_noise(splits[2], (FF, D), FF ** -0.5, 0.0546875, ((0, 4), (1, 4)), (0, 1, 4, 2.0)),
    }


def reference(tokens, w_in, w_out):
    state = tokens
    for step in range(STEPS):
        pre = jnp.dot(state, w_in, preferred_element_type=jnp.float32)
        activ = jax.nn.gelu(pre, approximate=True).astype(jnp.bfloat16)
        term = jnp.dot(activ, w_out, preferred_element_type=jnp.float32)
        state = (state.astype(jnp.float32) + term).astype(jnp.bfloat16)
    return state
```

```python
import jax
import jax.numpy as jnp
from jax import lax
from jax.experimental import pallas as pl
from jax.experimental.pallas import tpu as pltpu
from jax.sharding import PartitionSpec as P

STEPS = 2
PIECES = 2
COLS = 4
bf16, f32 = jnp.bfloat16, jnp.float32


def plain(tokens, w_in, w_out):
    row_dev = tokens.shape[0]
    where = lax.axis_index("hidden")
    full = lax.all_gather(tokens, "hidden", axis=0, tiled=True)
    latest = tokens
    for step in range(STEPS):
        pre = jnp.dot(full, w_in, preferred_element_type=f32)
        summed = lax.psum(pre.astype(bf16), "width").astype(f32)
        activ = jax.nn.gelu(summed, approximate=True).astype(bf16)
        mine_sum = lax.psum_scatter(
            jnp.dot(activ, w_out, preferred_element_type=f32).astype(bf16),
            "hidden",
            scatter_dimension=0,
            tiled=True,
        ).astype(f32)
        mine_old = lax.dynamic_slice_in_dim(full, where * row_dev, row_dev, 0)
        latest = (mine_old.astype(f32) + mine_sum).astype(bf16)
        if step + 1 < STEPS:
            full = lax.all_gather(latest, "hidden", axis=0, tiled=True)
    return latest


def swap(x, axis, n, mask):
    return lax.ppermute(x, axis, [(i, i ^ mask) for i in range(n)])


def stage(products, loads, name, behind=()):
    arrays = []
    for array, _, _ in loads:
        if not any(array is a for a in arrays):
            arrays.append(array)
    flat = [r for pair in products for r in pair]
    n_p, n_a, n_l = len(flat), len(arrays), len(loads)
    which = [next(i for i, a in enumerate(arrays) if a is array) for array, _, _ in loads]

    def kernel(*refs):
        given, hbm = refs[:n_p], refs[n_p : n_p + n_a]
        out = refs[n_p + n_a + len(behind) :]
        result = out[0] if products else None
        out = out[1:] if products else out
        held, sems = out[:n_l], out[n_l:]
        core = lax.rem(lax.axis_index("width"), 2)
        copies = []
        for i, (array, rows, cols) in enumerate(loads):
            index = []
            for (size, start, per), full in zip((rows, cols), array.shape):
                if per:
                    half = core if per > 0 else 1 - core
                    start = pl.multiple_of(half * (full // 2) + start, 128)
                index.append(pl.ds(start, size))
            copies.append(pltpu.make_async_copy(hbm[which[i]].at[tuple(index)], held[i], sems[0].at[i]))
        for copy in copies:
            copy.start()
        if products:
            total = None
            for i in range(0, n_p, 2):
                part = jnp.dot(given[i][...], given[i + 1][...], preferred_element_type=f32)
                total = part if total is None else total + part
            result[...] = total.astype(result.dtype)
        for copy in copies:
            copy.wait()

    shapes = [pltpu.VMEM((r[0], c[0]), a.dtype) for a, r, c in loads]
    if products:
        shapes = [jax.ShapeDtypeStruct((flat[0].shape[0], flat[1].shape[1]), bf16)] + shapes
    vmem = pl.BlockSpec(memory_space=pltpu.VMEM)
    got = pl.pallas_call(
        kernel,
        out_shape=shapes,
        in_specs=[vmem] * n_p + [pl.BlockSpec(memory_space=pltpu.HBM)] * n_a + [pl.BlockSpec(memory_space=pl.ANY)] * len(behind),
        out_specs=[vmem] * len(shapes),
        scratch_shapes=[pltpu.SemaphoreType.DMA((n_l,))] if loads else [],
        compiler_params=pltpu.CompilerParams(vmem_limit_bytes=3 * 2**20),
        cost_estimate=pl.CostEstimate(
            flops=sum(2 * flat[i].shape[0] * flat[i + 1].size for i in range(0, n_p, 2)),
            bytes_accessed=sum(2 * r[0] * c[0] for _, r, c in loads),
            transcendentals=0,
        ),
        name=name,
    )(*flat, *[pltpu.with_memory_space_constraint(a, pltpu.HBM) for a in arrays], *behind)
    return (got[0], list(got[1:])) if products else (None, list(got))


def gather(block, nz):
    return jnp.concatenate([block] + [swap(block, "hidden", nz, k) for k in range(1, nz)], 0)


def tuned(nz, nw, tokens, w_in, w_out):
    rows, d = tokens.shape
    f = w_in.shape[1]
    piece, cols = f // 2 // PIECES, d // COLS

    def up(j, per):
        return (w_in, (d, 0, 0), (piece, j * piece, per))

    def down(n):
        return [(w_out, (f // 2, 0, per), (cols, n * cols, 0)) for per in (1, -1)]

    def after(sent, kept):
        chip = (kept.astype(f32) + swap(sent, "width", nw, 1).astype(f32)).astype(bf16)
        total = chip.astype(f32) + swap(chip, "width", nw, 2).astype(f32)
        return jax.nn.gelu(total, approximate=True).astype(bf16)

    def scattered(part, old):
        total = part[:rows].astype(f32)
        for k in range(1, nz):
            total = total + swap(part[k * rows : (k + 1) * rows], "hidden", nz, k).astype(f32)
        return (old.astype(f32) + total).astype(bf16)

    x = gather(tokens, nz)
    old = [tokens[:, n * cols : (n + 1) * cols] for n in range(COLS)]

    _, (t0, m0) = stage([], [up(0, -1), up(0, 1)], "load_up")
    p_t0, (t1,) = stage([(x, t0)], [up(1, -1)], "up_t0")
    p_m0, (m1,) = stage([(x, m0)], [up(1, 1)], "up_m0", [p_t0])
    p_t1, wo0 = stage([(x, t1)], down(0), "up_t1", [p_m0])
    p_m1, wo1 = stage([(x, m1)], down(1), "up_m1", [p_t1])
    a0 = after(p_t0, p_m0)
    a1 = after(p_t1, p_m1)
    _, wo2 = stage([], down(2), "load_down", [p_m1])
    mine = jnp.concatenate([a0, a1], 1)
    other = jnp.concatenate([swap(a0, "width", nw, 1), swap(a1, "width", nw, 1)], 1)
    q0, _ = stage([(mine, wo0[0]), (other, wo0[1])], [], "down_0", [wo2[0]])
    q1, wo3 = stage([(mine, wo1[0]), (other, wo1[1])], down(3), "down_1", [q0])
    q2, (t0,) = stage([(mine, wo2[0]), (other, wo2[1])], [up(0, -1)], "down_2", [q1])
    q3, _ = stage([(mine, wo3[0]), (other, wo3[1])], [], "down_3", [q2])
    old = [scattered(q, o) for q, o in zip((q0, q1, q2, q3), old)]
    x = jnp.concatenate([gather(o, nz) for o in old], 1)

    p_t0, _ = stage([(x, t0)], [], "up_t0")
    p_m0, _ = stage([(x, m0)], [], "up_m0", [p_t0])
    p_t1, _ = stage([(x, t1)], [], "up_t1", [p_m0])
    p_m1, _ = stage([(x, m1)], [], "up_m1", [p_t1])
    a0 = after(p_t0, p_m0)
    a1 = after(p_t1, p_m1)
    _, wo01 = stage([], down(0) + down(1), "load_down", [p_m1])
    wo0, wo1 = wo01[:2], wo01[2:]
    mine = jnp.concatenate([a0, a1], 1)
    other = jnp.concatenate([swap(a0, "width", nw, 1), swap(a1, "width", nw, 1)], 1)
    new, last = [], wo01[0]
    for n, wo in ((2, wo2), (3, wo3), (0, wo0), (1, wo1)):
        last, _ = stage([(mine, wo[0]), (other, wo[1])], [], f"down_{n}", [last])
        new.append((n, scattered(last, old[n])))
    return jnp.concatenate([v for _, v in sorted(new, key=lambda item: item[0])], 1)


def solution(mesh):
    placed = (P(("groups", "hidden"), "width"), P("width", "hidden"), P("hidden", "width"))
    nz, nw = mesh.shape["hidden"], mesh.shape["width"]

    def local(tokens, w_in, w_out):
        fits = nz == 4 and nw == 4 and w_in.shape[1] % (256 * PIECES) == 0
        return tuned(nz, nw, tokens, w_in, w_out) if fits else plain(tokens, w_in, w_out)

    return jax.shard_map(
        local,
        mesh=mesh,
        in_specs=placed,
        out_specs=P(("groups", "hidden"), "width"),
        check_vma=False,
    )
```

```python
import jax
import jax.numpy as jnp
from jax import lax
from jax.experimental import pallas as pl
from jax.experimental.pallas import tpu as pltpu
from jax.sharding import PartitionSpec as P

STEPS = 2
PIECES = 2
BLOCKS = 2
bf16, f32 = jnp.bfloat16, jnp.float32


def plain(tokens, w_in, w_out):
    row_dev = tokens.shape[0]
    where = lax.axis_index("hidden")
    full = lax.all_gather(tokens, "hidden", axis=0, tiled=True)
    latest = tokens
    for step in range(STEPS):
        pre = jnp.dot(full, w_in, preferred_element_type=f32)
        summed = lax.psum(pre.astype(bf16), "width").astype(f32)
        activ = jax.nn.gelu(summed, approximate=True).astype(bf16)
        mine_sum = lax.psum_scatter(
            jnp.dot(activ, w_out, preferred_element_type=f32).astype(bf16),
            "hidden",
            scatter_dimension=0,
            tiled=True,
        ).astype(f32)
        mine_old = lax.dynamic_slice_in_dim(full, where * row_dev, row_dev, 0)
        latest = (mine_old.astype(f32) + mine_sum).astype(bf16)
        if step + 1 < STEPS:
            full = lax.all_gather(latest, "hidden", axis=0, tiled=True)
    return latest


def swap(x, axis, n, mask):
    return lax.ppermute(x, axis, [(i, i ^ mask) for i in range(n)])


def stage(products, loads, name, behind=(), add=None, dtype=bf16):
    arrays = []
    for array, _, _ in loads:
        if not any(array is a for a in arrays):
            arrays.append(array)
    given = [a for x, w in products for a in (x, *w)] + ([] if add is None else [add])
    n_g, n_a, n_l = len(given), len(arrays), BLOCKS * len(loads)
    which = [next(i for i, a in enumerate(arrays) if a is array) for array, _, _ in loads]
    width = w_width = 0
    if products:
        w_width = products[0][1][0].shape[1]
        width = BLOCKS * w_width

    def kernel(*refs):
        refs_in, hbm = refs[:n_g], refs[n_g : n_g + n_a]
        out = refs[n_g + n_a + len(behind) :]
        result = out[0] if products else None
        out = out[1:] if products else out
        held, sems = out[:n_l], out[n_l:]
        core = lax.rem(lax.axis_index("width"), 2)
        copies = []
        for i, (array, rows, cols) in enumerate(loads):
            size = cols[0] // BLOCKS
            for b in range(BLOCKS):
                index = []
                for (extent, start, per), full in zip((rows, (size, cols[1] + b * size, cols[2])), array.shape):
                    if per:
                        half = core if per > 0 else 1 - core
                        start = pl.multiple_of(half * (full // 2) + start, 128)
                    index.append(pl.ds(start, extent))
                slot = i * BLOCKS + b
                copies.append(pltpu.make_async_copy(hbm[which[i]].at[tuple(index)], held[slot], sems[0].at[slot]))
        for copy in copies:
            copy.start()
        if products:

            @pl.when(core < 2)
            def _():
                for b in range(BLOCKS):
                    columns = slice(b * w_width, (b + 1) * w_width)
                    total = None if add is None else refs_in[-1][:, columns]
                    for p in range(len(products)):
                        x, w = refs_in[p * (1 + BLOCKS)], refs_in[p * (1 + BLOCKS) + 1 + b]
                        part = jnp.dot(x[...], w[...], preferred_element_type=f32)
                        total = part if total is None else total + part
                    result[:, columns] = total.astype(result.dtype)

        for copy in copies:
            copy.wait()

    shapes = [pltpu.VMEM((r[0], c[0] // BLOCKS), a.dtype) for a, r, c in loads for _ in range(BLOCKS)]
    if products:
        shapes = [jax.ShapeDtypeStruct((given[0].shape[0], width), dtype)] + shapes
    vmem, hbm, anywhere = (pl.BlockSpec(memory_space=m) for m in (pltpu.VMEM, pltpu.HBM, pl.ANY))
    got = pl.pallas_call(
        kernel,
        out_shape=shapes,
        in_specs=[vmem] * n_g + [hbm] * n_a + [anywhere] * len(behind),
        out_specs=[vmem] * len(shapes),
        scratch_shapes=[pltpu.SemaphoreType.DMA((n_l,))] if loads else [],
        compiler_params=pltpu.CompilerParams(vmem_limit_bytes=2 * 2**20),
        cost_estimate=pl.CostEstimate(flops=1000, bytes_accessed=1000, transcendentals=0),
        name=name,
    )(*given, *[pltpu.with_memory_space_constraint(a, pltpu.HBM) for a in arrays], *behind)
    result, blocks = (got[0], got[1:]) if products else (None, got)
    return result, [list(blocks[i * BLOCKS : (i + 1) * BLOCKS]) for i in range(len(loads))]


def gather(block, nz):
    return jnp.concatenate([block] + [swap(block, "hidden", nz, k) for k in range(1, nz)], 0)


def tuned(nz, nw, tokens, w_in, w_out):
    rows, d = tokens.shape
    f = w_in.shape[1]
    piece = f // 2 // PIECES

    def up(j, per):
        return (w_in, (d, 0, 0), (piece, j * piece, per))

    def down(j, per):
        return (w_out, (piece, j * piece, per), (d, 0, 0))

    def chip_sum(sent, kept):
        return (kept.astype(f32) + swap(sent, "width", nw, 1).astype(f32)).astype(bf16)

    def activation(chip):
        total = chip.astype(f32) + swap(chip, "width", nw, 2).astype(f32)
        return jax.nn.gelu(total, approximate=True).astype(bf16)

    def scattered(part, old):
        total = part[:rows].astype(f32)
        for k in range(nz - 1, 0, -1):
            total = total + swap(part[k * rows : (k + 1) * rows], "hidden", nz, k).astype(f32)
        return (old.astype(f32) + total).astype(bf16)

    state = tokens
    x = gather(state, nz)
    _, (t0,) = stage([], [up(0, -1)], "load_t0")
    s_t0, (m0,) = stage([(x, t0)], [up(0, 1)], "up_t0")
    s_m0, (t1,) = stage([(x, m0)], [up(1, -1)], "up_m0", [s_t0])
    c0 = chip_sum(s_t0, s_m0)
    s_t1, (m1,) = stage([(x, t1)], [up(1, 1)], "up_t1", [c0])
    s_m1, (d_m0, d_m1) = stage([(x, m1)], [down(0, 1), down(1, 1)], "up_m1", [s_t1])
    for step in range(STEPS):
        c1 = chip_sum(s_t1, s_m1)
        mine0 = activation(c0)
        q, (d_t0, d_t1) = stage([(mine0, d_m0)], [down(0, -1), down(1, -1)], "down_m0", [c1], None, f32)
        other0 = swap(mine0, "width", nw, 1)
        mine1 = activation(c1)
        q, _ = stage([(other0, d_t0), (mine1, d_m1)], [], "down_t0_m1", [], q, f32)
        other1 = swap(mine1, "width", nw, 1)
        q, _ = stage([(other1, d_t1)], [], "down_t1", [], q)
        if step + 1 < STEPS:
            _, (t0,) = stage([], [up(0, -1)], "load_t0", [q])
        state = scattered(q, state)
        if step + 1 < STEPS:
            _, (m0,) = stage([], [up(0, 1)], "load_m0", [state])
            x = gather(state, nz)
            s_t0, (t1,) = stage([(x, t0)], [up(1, -1)], "up_t0", [m0[0]])
            s_m0, (d_m0,) = stage([(x, m0)], [down(0, 1)], "up_m0", [s_t0])
            c0 = chip_sum(s_t0, s_m0)
            s_t1, (d_m1,) = stage([(x, t1)], [down(1, 1)], "up_t1", [c0])
            s_m1, _ = stage([(x, m1)], [], "up_m1", [s_t1])
    return state


def solution(mesh):
    placed = (P(("groups", "hidden"), "width"), P("width", "hidden"), P("hidden", "width"))
    nz, nw = mesh.shape["hidden"], mesh.shape["width"]

    def local(tokens, w_in, w_out):
        fits = nz == 4 and nw == 4 and w_in.shape[1] % (256 * PIECES) == 0
        return tuned(nz, nw, tokens, w_in, w_out) if fits else plain(tokens, w_in, w_out)

    return jax.shard_map(
        local,
        mesh=mesh,
        in_specs=placed,
        out_specs=P(("groups", "hidden"), "width"),
        check_vma=False,
    )
```

```python
import jax
import jax.numpy as jnp
from jax import lax
from jax.experimental import pallas as pl
from jax.experimental.pallas import tpu as pltpu
from jax.sharding import PartitionSpec as P

STEPS = 2
BLOCKS = 8
EARLY = 4
bf16, f32 = jnp.bfloat16, jnp.float32


def plain(tokens, w_in, w_out):
    row_dev = tokens.shape[0]
    where = lax.axis_index("hidden")
    full = lax.all_gather(tokens, "hidden", axis=0, tiled=True)
    latest = tokens
    for step in range(STEPS):
        pre = jnp.dot(full, w_in, preferred_element_type=f32)
        summed = lax.psum(pre.astype(bf16), "width").astype(f32)
        activ = jax.nn.gelu(summed, approximate=True).astype(bf16)
        mine_sum = lax.psum_scatter(
            jnp.dot(activ, w_out, preferred_element_type=f32).astype(bf16),
            "hidden",
            scatter_dimension=0,
            tiled=True,
        ).astype(f32)
        mine_old = lax.dynamic_slice_in_dim(full, where * row_dev, row_dev, 0)
        latest = (mine_old.astype(f32) + mine_sum).astype(bf16)
        if step + 1 < STEPS:
            full = lax.all_gather(latest, "hidden", axis=0, tiled=True)
    return latest


def swap(x, axis, n, mask):
    return lax.ppermute(x, axis, [(i, i ^ mask) for i in range(n)])


def stage(products, loads, name, behind=(), add=None, dtype=bf16, carry=None, over=()):
    given = [a for x, w in products for a in (x, *w)] + [a for a in (add, carry) if a is not None]
    copied = [(array, dim, per, b) for array, dim, per, first, last in loads for b in range(first, last)]
    n_g, n_a, n_l = len(given), len(loads), len(copied)
    n_b = len(products[0][1]) if products else 0
    wide = products[0][1][0].shape[1] if products else 0
    source = [i for i, (_, _, _, first, last) in enumerate(loads) for _ in range(first, last)]

    def size(array, dim):
        rows, cols = (n // 2 if k == dim else n for k, n in enumerate(array.shape))
        return rows, cols // BLOCKS

    def kernel(*refs):
        refs_in, hbm = refs[:n_g], refs[n_g : n_g + n_a]
        out = list(refs[n_g + n_a + len(behind) + len(over) :])
        result = out.pop(0) if products else None
        carried = out.pop(0) if carry is not None else None
        held, sems = out[:n_l], out[n_l:]
        core = lax.rem(lax.axis_index("width"), 2)
        copies = []
        for i, (array, dim, per, b) in enumerate(copied):
            rows, cols = size(array, dim)
            half = core if per > 0 else 1 - core
            top, left = (half * rows, b * cols) if dim == 0 else (0, half * (cols * BLOCKS) + b * cols)
            index = (pl.ds(pl.multiple_of(top, 128), rows), pl.ds(pl.multiple_of(left, 128), cols))
            copies.append(pltpu.make_async_copy(hbm[source[i]].at[index], held[i], sems[0].at[i]))
        for copy in copies:
            copy.start()
        if carry is not None:
            carried[...] = refs_in[-1][...]
        if products:

            @pl.when(core < 2)
            def _():
                for b in range(n_b):
                    columns = slice(b * wide, (b + 1) * wide)
                    total = None if add is None else refs_in[len(products) * (1 + n_b)][:, columns]
                    for p in range(len(products)):
                        x, w = refs_in[p * (1 + n_b)], refs_in[p * (1 + n_b) + 1 + b]
                        part = jnp.dot(x[...], w[...], preferred_element_type=f32)
                        total = part if total is None else total + part
                    result[:, columns] = total.astype(result.dtype)

        for copy in copies:
            copy.wait()

    shapes = [pltpu.VMEM(size(array, dim), array.dtype) for array, dim, _, _ in copied]
    if carry is not None:
        shapes = [jax.ShapeDtypeStruct(carry.shape, carry.dtype)] + shapes
    if products:
        shapes = [jax.ShapeDtypeStruct((given[0].shape[0], n_b * wide), dtype)] + shapes
    vmem, hbm, anywhere = (pl.BlockSpec(memory_space=m) for m in (pltpu.VMEM, pltpu.HBM, pl.ANY))
    got = pl.pallas_call(
        kernel,
        out_shape=shapes,
        in_specs=[vmem] * n_g + [hbm] * n_a + [anywhere] * len(behind) + [vmem] * len(over),
        out_specs=[vmem] * len(shapes),
        input_output_aliases={n_g + n_a + len(behind) + i: len(shapes) - n_l + i for i in range(len(over))},
        scratch_shapes=[pltpu.SemaphoreType.DMA((n_l,))] if loads else [],
        compiler_params=pltpu.CompilerParams(vmem_limit_bytes=2 * 2**20),
        cost_estimate=pl.CostEstimate(flops=1000, bytes_accessed=1000, transcendentals=0),
        name=name,
    )(*given, *[pltpu.with_memory_space_constraint(load[0], pltpu.HBM) for load in loads], *behind, *over)
    got = list(got)
    lead = [got.pop(0) for there in (products, carry is not None) if there]
    return *lead, got


def gather(block, nz):
    return jnp.concatenate([block] + [swap(block, "hidden", nz, k) for k in range(1, nz)], 0)


def tuned(nz, nw, tokens, w_in, w_out):
    rows, d = tokens.shape
    def load(array, dim, per, first=0, last=BLOCKS):
        return (array, dim, per, first, last)

    def scattered(part, old, total):
        for k in range(nz - 1, 0, -1):
            total = total + swap(part[k * rows : (k + 1) * rows], "hidden", nz, k).astype(f32)
        return (old.astype(f32) + total).astype(bf16)

    state = tokens
    x = gather(state, nz)
    (other_in,) = stage([], [load(w_in, 1, -1)], "load_other_in")
    for step in range(STEPS):
        first, last = step == 0, step + 1 == STEPS
        sent, got = stage([(x, other_in)], [load(w_in, 1, 1)] if first else [], "up_other")
        mine_in = got if first else mine_in
        kept, got = stage([(x, mine_in)], [load(w_out, 0, 1)] if first else [], "up_mine", [sent])
        mine_out = got if first else mine_out
        chip = (kept.astype(f32) + swap(sent, "width", nw, 1).astype(f32)).astype(bf16)
        across = swap(chip, "width", nw, 2)
        chip, other_out = stage([], [load(w_out, 0, -1)], "load_other_out", carry=chip, over=other_in)
        total = chip.astype(f32) + across.astype(f32)
        mine = jax.nn.gelu(total, approximate=True).astype(bf16)
        other = swap(mine, "width", nw, 1)
        part, _ = stage([(mine, mine_out)], [], "down_mine", [], None, f32)
        part, _ = stage([(other, other_out)], [], "down_other", [], part)
        if last:
            state = scattered(part, state, part[:rows].astype(f32))
        else:
            half = [load(w_in, 1, -1, 0, EARLY)], [load(w_in, 1, -1, EARLY, BLOCKS)]
            old, got = stage([], half[0], "load_other_in", [part], carry=state, over=other_out[:EARLY])
            state = scattered(part, old, part[:rows].astype(f32))
            other_in = got + stage([], half[1], "load_other_in", [state], over=other_out[EARLY:])[0]
            x = gather(state, nz)
    return state


def solution(mesh):
    placed = (P(("groups", "hidden"), "width"), P("width", "hidden"), P("hidden", "width"))
    nz, nw = mesh.shape["hidden"], mesh.shape["width"]

    def local(tokens, w_in, w_out):
        d = tokens.shape[1]
        fits = nz == 4 and nw == 4 and w_in.shape[1] == 2 * d and d % (128 * BLOCKS) == 0
        return tuned(nz, nw, tokens, w_in, w_out) if fits else plain(tokens, w_in, w_out)

    return jax.shard_map(
        local,
        mesh=mesh,
        in_specs=placed,
        out_specs=P(("groups", "hidden"), "width"),
        check_vma=False,
    )
```

```python
import jax
import jax.numpy as jnp
from jax import lax
from jax.experimental import pallas as pl
from jax.experimental.pallas import tpu as pltpu
from jax.sharding import PartitionSpec as P

STEPS = 2
BLOCKS = 8
EARLY = 4
WITH_UP = 4
bf16, f32 = jnp.bfloat16, jnp.float32


def plain(tokens, w_in, w_out):
    row_dev = tokens.shape[0]
    where = lax.axis_index("hidden")
    full = lax.all_gather(tokens, "hidden", axis=0, tiled=True)
    latest = tokens
    for step in range(STEPS):
        pre = jnp.dot(full, w_in, preferred_element_type=f32)
        summed = lax.psum(pre.astype(bf16), "width").astype(f32)
        activ = jax.nn.gelu(summed, approximate=True).astype(bf16)
        mine_sum = lax.psum_scatter(
            jnp.dot(activ, w_out, preferred_element_type=f32).astype(bf16),
            "hidden",
            scatter_dimension=0,
            tiled=True,
        ).astype(f32)
        mine_old = lax.dynamic_slice_in_dim(full, where * row_dev, row_dev, 0)
        latest = (mine_old.astype(f32) + mine_sum).astype(bf16)
        if step + 1 < STEPS:
            full = lax.all_gather(latest, "hidden", axis=0, tiled=True)
    return latest


def swap(x, axis, n, mask):
    return lax.ppermute(x, axis, [(i, i ^ mask) for i in range(n)])


def stage(products, loads, name, behind=(), add=None, dtype=bf16, carry=None, over=()):
    given = [a for x, w in products for a in (x, *w)] + [a for a in (add, carry) if a is not None]
    copied = [(array, dim, per, b) for array, dim, per, first, last in loads for b in range(first, last)]
    n_g, n_a, n_l = len(given), len(loads), len(copied)
    n_b = len(products[0][1]) if products else 0
    wide = products[0][1][0].shape[1] if products else 0
    source = [i for i, (_, _, _, first, last) in enumerate(loads) for _ in range(first, last)]

    def size(array, dim):
        rows, cols = (n // 2 if k == dim else n for k, n in enumerate(array.shape))
        return rows, cols // BLOCKS

    def kernel(*refs):
        refs_in, hbm = refs[:n_g], refs[n_g : n_g + n_a]
        out = list(refs[n_g + n_a + len(behind) + len(over) :])
        result = out.pop(0) if products else None
        carried = out.pop(0) if carry is not None else None
        held, sems = out[:n_l], out[n_l:]
        core = lax.rem(lax.axis_index("width"), 2)
        copies = []
        for i, (array, dim, per, b) in enumerate(copied):
            rows, cols = size(array, dim)
            half = core if per > 0 else 1 - core
            top, left = (half * rows, b * cols) if dim == 0 else (0, half * (cols * BLOCKS) + b * cols)
            index = (pl.ds(pl.multiple_of(top, 128), rows), pl.ds(pl.multiple_of(left, 128), cols))
            copies.append(pltpu.make_async_copy(hbm[source[i]].at[index], held[i], sems[0].at[i]))
        for copy in copies:
            copy.start()
        if carry is not None:
            carried[...] = refs_in[-1][...]
        if products:

            @pl.when(core < 2)
            def _():
                for b in range(n_b):
                    columns = slice(b * wide, (b + 1) * wide)
                    total = None if add is None else refs_in[len(products) * (1 + n_b)][:, columns]
                    for p in range(len(products)):
                        x, w = refs_in[p * (1 + n_b)], refs_in[p * (1 + n_b) + 1 + b]
                        part = jnp.dot(x[...], w[...], preferred_element_type=f32)
                        total = part if total is None else total + part
                    result[:, columns] = total.astype(result.dtype)

        for copy in copies:
            copy.wait()

    shapes = [pltpu.VMEM(size(array, dim), array.dtype) for array, dim, _, _ in copied]
    if carry is not None:
        shapes = [jax.ShapeDtypeStruct(carry.shape, carry.dtype)] + shapes
    if products:
        shapes = [jax.ShapeDtypeStruct((given[0].shape[0], n_b * wide), dtype)] + shapes
    vmem, hbm, anywhere = (pl.BlockSpec(memory_space=m) for m in (pltpu.VMEM, pltpu.HBM, pl.ANY))
    got = pl.pallas_call(
        kernel,
        out_shape=shapes,
        in_specs=[vmem] * n_g + [hbm] * n_a + [anywhere] * len(behind) + [vmem] * len(over),
        out_specs=[vmem] * len(shapes),
        input_output_aliases={n_g + n_a + len(behind) + i: len(shapes) - n_l + i for i in range(len(over))},
        scratch_shapes=[pltpu.SemaphoreType.DMA((n_l,))] if loads else [],
        compiler_params=pltpu.CompilerParams(vmem_limit_bytes=2 * 2**20),
        cost_estimate=pl.CostEstimate(flops=1000, bytes_accessed=1000, transcendentals=0),
        name=name,
    )(*given, *[pltpu.with_memory_space_constraint(load[0], pltpu.HBM) for load in loads], *behind, *over)
    got = list(got)
    lead = [got.pop(0) for there in (products, carry is not None) if there]
    return *lead, got


def gather(block, nz):
    return jnp.concatenate([block] + [swap(block, "hidden", nz, k) for k in range(1, nz)], 0)


def tuned(nz, nw, tokens, w_in, w_out):
    rows, d = tokens.shape
    def load(array, dim, per, first=0, last=BLOCKS):
        return (array, dim, per, first, last)

    def scattered(part, old, total):
        for k in range(nz - 1, 0, -1):
            total = total + swap(part[k * rows : (k + 1) * rows], "hidden", nz, k).astype(f32)
        return (old.astype(f32) + total).astype(bf16)

    def rows_of(x):
        far = swap(x, "hidden", nz, 2)
        x, first = stage([], [load(w_in, 1, -1, 0, BLOCKS // 2)], "load_other_in", carry=x)
        near = swap(jnp.concatenate([x, far], 0), "hidden", nz, 1)
        x, second = stage([], [load(w_in, 1, -1, BLOCKS // 2, BLOCKS)], "load_other_in", [far], carry=x)
        return jnp.concatenate([x, near[:rows], far, near[rows:]], 0), first + second

    state = tokens
    x, other_in = rows_of(state)
    for step in range(STEPS):
        first, last = step == 0, step + 1 == STEPS
        sent, got = stage([(x, other_in)], [load(w_in, 1, 1)] if first else [], "up_other")
        mine_in = got if first else mine_in
        kept, got = stage([(x, mine_in)], [load(w_out, 0, 1, 0, WITH_UP)] if first else [], "up_mine", [sent])
        mine_out = got if first else mine_out
        chip = (kept.astype(f32) + swap(sent, "width", nw, 1).astype(f32)).astype(bf16)
        across = swap(chip, "width", nw, 2)
        begun = WITH_UP if first else BLOCKS
        wanted = [load(w_out, 0, 1, begun, BLOCKS)] * (begun < BLOCKS) + [load(w_out, 0, -1, 0, begun)]
        chip, got = stage([], wanted, "load_out", carry=chip, over=other_in)
        mine_out, other_out = mine_out + got[: BLOCKS - begun], got[BLOCKS - begun :]
        total = chip.astype(f32) + across.astype(f32)
        mine = jax.nn.gelu(total, approximate=True).astype(bf16)
        other = swap(mine, "width", nw, 1)
        part, got = stage([(mine, mine_out)], [load(w_out, 0, -1, begun, BLOCKS)] if first else [], "down_mine", [], None, f32)
        part, _ = stage([(other, other_out + got)], [], "down_other", [], part)
        other_out = other_out + got
        if last:
            state = scattered(part, state, part[:rows].astype(f32))
        else:
            half = [load(w_in, 1, -1, 0, EARLY)], [load(w_in, 1, -1, EARLY, BLOCKS)]
            old, got = stage([], half[0], "load_other_in", [part], carry=state, over=other_out[:EARLY])
            state = scattered(part, old, part[:rows].astype(f32))
            other_in = got + stage([], half[1], "load_other_in", [state], over=other_out[EARLY:])[0]
            x = gather(state, nz)
    return state


def solution(mesh):
    placed = (P(("groups", "hidden"), "width"), P("width", "hidden"), P("hidden", "width"))
    nz, nw = mesh.shape["hidden"], mesh.shape["width"]

    def local(tokens, w_in, w_out):
        d = tokens.shape[1]
        fits = nz == 4 and nw == 4 and w_in.shape[1] == 2 * d and d % (128 * BLOCKS) == 0
        return tuned(nz, nw, tokens, w_in, w_out) if fits else plain(tokens, w_in, w_out)

    return jax.shard_map(
        local,
        mesh=mesh,
        in_specs=placed,
        out_specs=P(("groups", "hidden"), "width"),
        check_vma=False,
    )
```

```python
import jax
import jax.numpy as jnp
from jax import lax
from jax.experimental import pallas as pl
from jax.experimental.pallas import tpu as pltpu
from jax.sharding import PartitionSpec as P

STEPS = 2
BLOCKS = 8
HALF = BLOCKS // 2
bf16, f32 = jnp.bfloat16, jnp.float32


def plain(tokens, w_in, w_out):
    row_dev = tokens.shape[0]
    where = lax.axis_index("hidden")
    full = lax.all_gather(tokens, "hidden", axis=0, tiled=True)
    latest = tokens
    for step in range(STEPS):
        pre = jnp.dot(full, w_in, preferred_element_type=f32)
        summed = lax.psum(pre.astype(bf16), "width").astype(f32)
        activ = jax.nn.gelu(summed, approximate=True).astype(bf16)
        mine_sum = lax.psum_scatter(
            jnp.dot(activ, w_out, preferred_element_type=f32).astype(bf16),
            "hidden",
            scatter_dimension=0,
            tiled=True,
        ).astype(f32)
        mine_old = lax.dynamic_slice_in_dim(full, where * row_dev, row_dev, 0)
        latest = (mine_old.astype(f32) + mine_sum).astype(bf16)
        if step + 1 < STEPS:
            full = lax.all_gather(latest, "hidden", axis=0, tiled=True)
    return latest


def swap(x, axis, n, mask):
    return lax.ppermute(x, axis, [(i, i ^ mask) for i in range(n)])


def stage(products, loads, name, behind=(), add=None, dtype=bf16, carry=None, over=()):
    given = [a for x, w in products for a in (x, *w)] + [a for a in (add, carry) if a is not None]
    copied = [(array, dim, per, b) for array, dim, per, first, last in loads for b in range(first, last)]
    n_g, n_a, n_l = len(given), len(loads), len(copied)
    n_b = len(products[0][1]) if products else 0
    wide = products[0][1][0].shape[1] if products else 0
    source = [i for i, (_, _, _, first, last) in enumerate(loads) for _ in range(first, last)]

    def size(array, dim):
        rows, cols = (n // 2 if k == dim else n for k, n in enumerate(array.shape))
        return rows, cols // BLOCKS

    def kernel(*refs):
        refs_in, hbm = refs[:n_g], refs[n_g : n_g + n_a]
        out = list(refs[n_g + n_a + len(behind) + len(over) :])
        result = out.pop(0) if products else None
        carried = out.pop(0) if carry is not None else None
        held, sems = out[:n_l], out[n_l:]
        core = lax.rem(lax.axis_index("width"), 2)
        copies = []
        for i, (array, dim, per, b) in enumerate(copied):
            rows, cols = size(array, dim)
            half = core if per > 0 else 1 - core
            top, left = (half * rows, b * cols) if dim == 0 else (0, half * (cols * BLOCKS) + b * cols)
            index = (pl.ds(pl.multiple_of(top, 128), rows), pl.ds(pl.multiple_of(left, 128), cols))
            copies.append(pltpu.make_async_copy(hbm[source[i]].at[index], held[i], sems[0].at[i]))
        for copy in copies:
            copy.start()
        if carry is not None:
            carried[...] = refs_in[-1][...]
        if products:

            @pl.when(core < 2)
            def _():
                for b in range(n_b):
                    columns = slice(b * wide, (b + 1) * wide)
                    total = None if add is None else refs_in[len(products) * (1 + n_b)][:, columns]
                    for p in range(len(products)):
                        x, w = refs_in[p * (1 + n_b)], refs_in[p * (1 + n_b) + 1 + b]
                        part = jnp.dot(x[...], w[...], preferred_element_type=f32)
                        total = part if total is None else total + part
                    result[:, columns] = total.astype(result.dtype)

        for copy in copies:
            copy.wait()

    shapes = [pltpu.VMEM(size(array, dim), array.dtype) for array, dim, _, _ in copied]
    if carry is not None:
        shapes = [jax.ShapeDtypeStruct(carry.shape, carry.dtype)] + shapes
    if products:
        shapes = [jax.ShapeDtypeStruct((given[0].shape[0], n_b * wide), dtype)] + shapes
    vmem, hbm, anywhere = (pl.BlockSpec(memory_space=m) for m in (pltpu.VMEM, pltpu.HBM, pl.ANY))
    got = pl.pallas_call(
        kernel,
        out_shape=shapes,
        in_specs=[vmem] * n_g + [hbm] * n_a + [anywhere] * len(behind) + [vmem] * len(over),
        out_specs=[vmem] * len(shapes),
        input_output_aliases={n_g + n_a + len(behind) + i: len(shapes) - n_l + i for i in range(len(over))},
        scratch_shapes=[pltpu.SemaphoreType.DMA((n_l,))] if loads else [],
        compiler_params=pltpu.CompilerParams(vmem_limit_bytes=2**19),
        cost_estimate=pl.CostEstimate(flops=1000, bytes_accessed=1000, transcendentals=0),
        name=name,
    )(*given, *[pltpu.with_memory_space_constraint(load[0], pltpu.HBM) for load in loads], *behind, *over)
    got = list(got)
    lead = [got.pop(0) for there in (products, carry is not None) if there]
    return *lead, got


def gather(block, nz):
    return jnp.concatenate([block] + [swap(block, "hidden", nz, k) for k in range(1, nz)], 0)


def tuned(nz, nw, tokens, w_in, w_out):
    rows, d = tokens.shape
    def load(array, dim, per, first=0, last=BLOCKS):
        return (array, dim, per, first, last)

    def scattered(part, old, total):
        for k in range(nz - 1, 0, -1):
            total = total + swap(part[k * rows : (k + 1) * rows], "hidden", nz, k).astype(f32)
        return (old.astype(f32) + total).astype(bf16)

    def rows_of(x):
        far = swap(x, "hidden", nz, 2)
        x, first = stage([], [load(w_in, 1, -1, 0, BLOCKS // 2)], "load_other_in", carry=x)
        near = swap(jnp.concatenate([x, far], 0), "hidden", nz, 1)
        x, second = stage([], [load(w_in, 1, -1, BLOCKS // 2, BLOCKS)], "load_other_in", [far], carry=x)
        return jnp.concatenate([x, near[:rows], far, near[rows:]], 0), first + second

    state = tokens
    x, other_in = rows_of(state)
    low, high = slice(0, HALF), slice(HALF, BLOCKS)
    for step in range(STEPS):
        first, last = step == 0, step + 1 == STEPS
        if first:
            sent, mine_in = stage([(x, other_in)], [load(w_in, 1, 1)], "up_other")
            kept, kept_out = stage([(x, mine_in)], [load(w_out, 0, 1, 0, HALF)], "up_mine", [sent])
        else:
            sent, got = stage([(x, other_in)], [load(w_in, 1, 1, 0, HALF)], "up_other", over=mine_out[high])
            mine_in = got + mine_in[high]
            kept, _ = stage([(x, mine_in)], [], "up_mine", [sent])
        chip = (kept.astype(f32) + swap(sent, "width", nw, 1).astype(f32)).astype(bf16)
        across = swap(chip, "width", nw, 2)
        wanted = [load(w_out, 0, 1, HALF, BLOCKS), load(w_out, 0, -1, 0, HALF)]
        chip, got = stage([], wanted, "load_out", carry=chip, over=mine_in[low] + other_in[low])
        mine_out, other_out = kept_out + got[low], got[high]
        total = chip.astype(f32) + across.astype(f32)
        mine = jax.nn.gelu(total, approximate=True).astype(bf16)
        other = swap(mine, "width", nw, 1)
        wanted = [load(w_out, 0, -1, HALF, BLOCKS)]
        part, got = stage([(mine, mine_out)], wanted, "down_mine", [], None, f32, over=other_in[high])
        other_out = other_out + got
        part, _ = stage([(other, other_out)], [], "down_other", [], part)
        if last:
            state = scattered(part, state, part[:rows].astype(f32))
        else:
            early, late = [load(w_in, 1, -1, 0, HALF)], [load(w_in, 1, -1, HALF, BLOCKS)]
            old, got = stage([], early, "load_other_in", [part], carry=state, over=other_out[low])
            state = scattered(part, old, part[:rows].astype(f32))
            other_in = got + stage([], late, "load_other_in", [state], over=other_out[high])[0]
            x = gather(state, nz)
    return state


def solution(mesh):
    placed = (P(("groups", "hidden"), "width"), P("width", "hidden"), P("hidden", "width"))
    nz, nw = mesh.shape["hidden"], mesh.shape["width"]

    def local(tokens, w_in, w_out):
        d = tokens.shape[1]
        fits = nz == 4 and nw == 4 and w_in.shape[1] == 2 * d and d % (128 * BLOCKS) == 0
        return tuned(nz, nw, tokens, w_in, w_out) if fits else plain(tokens, w_in, w_out)

    return jax.shard_map(
        local,
        mesh=mesh,
        in_specs=placed,
        out_specs=P(("groups", "hidden"), "width"),
        check_vma=False,
    )
```
